32 devices in a mesh: blk: 8 (over y, x, core), rep: 4 (over z).
Axes of the slice: x: 2, y: 2, z: 4, core: 2. Of those that a mesh axis runs over, the one named last changes fastest.
Arguments:
- p_tiles: float32 [8, 4, 4, 5, 128, 128], P('blk', 'rep'), may hold values from -1 to 1
- tasks: int32 [8, 4, 4, 3, 48], P('blk', 'rep'), may hold values from 0 to 19, as said below
Outputs:
- density_square: float32 [8, 4, 16, 128, 128], P('blk', 'rep')
The draws below stay inside these ranges and needn't reach their ends.
Inputs may be any that keep to these rules, and one draw needn't show every extreme that they name: Row 0 of tasks[b, r, s] indexes the 20 tiles of left_s, row 1 the 20 tiles of right_s, row 2 the target tile, where 16 marks an unused slot. Used slots come first in each list; each list has 12 to 48 used slots, and some list has all 48.
All inputs are finite; a program needn't handle non-finite values.
Results may differ from the reference program's by a relative error of at most 0.0003.
Values sent between devices are 32-bit elements; how exact they have to be, the bound alone decides.
No kernel may reach another device: no remote copies, remote signals or barrier semaphores. Data moves between devices by JAX's collectives and lax.ppermute only.
A program may use at most 192 MiB of HBM per device.

```python
import jax
import jax.numpy as jnp
from jax import lax

TILE = 128
TPS = 5
NTASK = 48
NC = 16
PANELS = 8
SLIVERS = 4
RSTEPS = 4
NT = 20
GROUP_TILES = 20


def draw_tasks(key, part):
    keys = jax.random.split(jax.random.fold_in(key, 17), 5)
    lists = (PANELS, SLIVERS, RSTEPS)
    shape = (PANELS, SLIVERS, RSTEPS, NTASK)
    lowest = NTASK // 4
    span = NTASK - lowest + 1
    raw = jax.random.randint(keys[0], lists, 0, span)
    live = lowest + raw * raw // span
    spot = jax.random.randint(keys[1], (), 0, PANELS * SLIVERS * RSTEPS)
    flat = live.reshape(-1)
    flat = jnp.where(jnp.arange(flat.shape[0]) == spot, NTASK, flat)
    live = flat.reshape(lists)
    first = jax.random.randint(keys[2], shape, 0, GROUP_TILES)
    second = jax.random.randint(keys[3], shape, 0, NT)
    target = jax.random.randint(keys[4], shape, 0, NC)
    slots = jnp.arange(NTASK)
    target = jnp.where(slots < live[..., None], target, NC)
    return jnp.stack([first, second, target], axis=3).astype(jnp.int32)


def levels(own_key, extent, shards, low, top_value):
    def one(position, shards_of):
        heights = jax.random.uniform(jax.random.fold_in(jax.random.fold_in(own_key, 6), position), (shards_of,), jnp.float32, low / len(shards), top_value / len(shards))
        return jnp.repeat(jnp.exp(heights), extent[position] // shards_of).reshape((-1,) + (1,) * (len(extent) - position - 1))

    factor_of = one(*shards[0])
    for cut in shards[1:]:
        factor_of = factor_of * one(*cut)
    return factor_of


def bell_draw(rng, shape, scale, most, pieces=(), kind=jnp.bfloat16):
    array = scale * jax.random.normal(rng, shape, jnp.float32)
    if pieces:
        array = array * levels(rng, shape, pieces, -0.22, 0.18)
    return jnp.clip(array, -most, most).astype(kind)


def setup_inputs(seed: int = 0) -> dict:
    splits = jax.random.split(jax.random.key(seed), 3)
    return {
        "p_tiles": bell_draw(splits[0], (PANELS, SLIVERS, RSTEPS, TPS, TILE, TILE), 0.18, 1.0, ((0, 8), (1, 4)), jnp.float32),
        "tasks": draw_tasks(jax.random.fold_in(splits[2], 71), 0),
    }


def reference(p_tiles, tasks):
    def one_device(index):
        panel_index = index // SLIVERS
        sliver_index = index % SLIVERS
        task_list = tasks[panel_index, sliver_index]
        summed = jnp.zeros((NC + 1, TILE, TILE), p_tiles.dtype)
        for step in range(RSTEPS):
            left_tiles = p_tiles[panel_index, :, step].reshape(GROUP_TILES, TILE, TILE)
            source = ((panel_index - step) % PANELS).astype(jnp.int32)
            right_tiles = p_tiles[source, sliver_index].reshape(NT, TILE, TILE)
            left_pick = left_tiles[task_list[step, 0]]
            right_pick = right_tiles[task_list[step, 1]]
            product = jnp.einsum("nij,njk->nik", left_pick, right_pick, precision=lax.Precision.HIGHEST)
            summed = summed + jax.ops.segment_sum(product, task_list[step, 2], num_segments=NC + 1)
        return summed[:NC]

    result = lax.map(one_device, jnp.arange(PANELS * SLIVERS, dtype=jnp.int32))
    return result.reshape(PANELS, SLIVERS, NC, TILE, TILE)
```

```python
import functools

import jax
import jax.numpy as jnp
from jax import lax
from jax.experimental import pallas as pl
from jax.experimental.pallas import tpu as pltpu
from jax.sharding import PartitionSpec as P

NC = 16
UNROLL = 4


def split(value):
    high = value.astype(jnp.bfloat16)
    low = (value - high.astype(jnp.float32)).astype(jnp.bfloat16)
    return high, low


def contract_kernel(n_left, first, last, tasks_ref, *refs):
    left_refs, right_ref = refs[:n_left], refs[n_left]
    rest = refs[n_left + 1 :]
    if first:
        out_ref, left_split, total, live = rest
    else:
        before_ref, out_ref, left_split, total, live = rest
    tile = right_ref.shape[-1]
    slots = tasks_ref.shape[-1]

    if first:
        total[...] = jnp.zeros_like(total)
    else:
        total[:NC] = before_ref[...]

    def pack(j, count):
        live[count] = j
        return count + jnp.where(tasks_ref[2, j] < NC, 1, 0)

    count = lax.fori_loop(0, slots, pack, 0)
    for extra in range(UNROLL):
        live[count + extra] = slots

    base = 0
    for ref in left_refs:
        for t in range(ref.shape[0]):
            high, low = split(ref[t])
            left_split[base + t, :, :tile] = high
            left_split[base + t, :, tile:] = low
        base += ref.shape[0]

    def some(i, carry):
        products, targets = [], []
        for u in range(UNROLL):
            j = live[i * UNROLL + u]
            dead = j >= slots
            at = jnp.where(dead, 0, j)
            high, low = split(right_ref[tasks_ref[1, at]])
            both = jnp.concatenate(
                [
                    jnp.concatenate([high, low], axis=1),
                    jnp.concatenate([high, jnp.zeros_like(low)], axis=1),
                ],
                axis=0,
            )
            wide = jnp.dot(
                left_split[tasks_ref[0, at]], both, preferred_element_type=jnp.float32
            )
            products.append(wide[:, :tile] + wide[:, tile:])
            targets.append(jnp.where(dead, NC, tasks_ref[2, at]))
        for product, target in zip(products, targets):
            total[target] += product
        return carry

    lax.fori_loop(0, (count + UNROLL - 1) // UNROLL, some, 0)
    out_ref[...] = total[:NC]


def contract(tasks, lefts, right, before):
    tile = right.shape[-1]
    n_tiles = sum(left.shape[0] for left in lefts)
    slots = tasks.shape[-1]
    vmem = pl.BlockSpec(memory_space=pltpu.VMEM)
    operands = [tasks, *lefts, right] + ([] if before is None else [before])
    return pl.pallas_call(
        functools.partial(contract_kernel, len(lefts), before is None, False),
        out_shape=jax.ShapeDtypeStruct((NC, tile, tile), jnp.float32),
        in_specs=[pl.BlockSpec(memory_space=pltpu.SMEM)] + [vmem] * (len(operands) - 1),
        out_specs=vmem,
        scratch_shapes=[
            pltpu.VMEM((n_tiles, tile, 2 * tile), jnp.bfloat16),
            pltpu.VMEM((NC + 1, tile, tile), jnp.float32),
            pltpu.SMEM((slots + UNROLL,), jnp.int32),
        ],
        compiler_params=pltpu.CompilerParams(vmem_limit_bytes=24 * 2**20),
        cost_estimate=pl.CostEstimate(
            flops=2 * 3 * slots * tile**3 // 4,
            bytes_accessed=4 * tile * tile * (n_tiles + right.shape[0] + 2 * NC),
            transcendentals=0,
        ),
    )(*operands)


def shift_pairs(count, by):
    return [(i, (i + by) % count) for i in range(count)]


def right_panels(own):
    panels, steps = lax.axis_size("blk"), own.shape[0]
    if steps != 4 or panels % 2:
        found = [own]
        for step in range(1, steps):
            found.append(lax.ppermute(own, "blk", shift_pairs(panels, step)))
        return found
    odd = lax.axis_index("blk") % 2 == 1
    two = lax.ppermute(own, "blk", shift_pairs(panels, 2))
    one = lax.ppermute(
        jnp.where(odd, two, own), "blk", [(i, i ^ 1) for i in range(panels)]
    )
    three = lax.ppermute(
        jnp.where(odd, own, two),
        "blk",
        [(i, (i + 3) % panels if i % 2 else i + 1) for i in range(panels)],
    )
    return [own, one, two, three]


def per_device(p_tiles, tasks):
    own = p_tiles[0, 0]
    lists = tasks[0, 0]
    steps, per, tile = own.shape[0], own.shape[1], own.shape[-1]
    slivers = lax.axis_size("rep")
    me = lax.axis_index("rep")

    away = lists[:, 0] // per - me
    spot = lists[:, 0] % per
    up_pairs = lambda far: [(i, i + 1) for i in range(far - 1, slivers - 1)]
    down_pairs = lambda far: [(i, i - 1) for i in range(slivers - far, 0, -1)]

    left = {}
    for step in range(steps):
        left[step, 0] = (own[step],)
    for far in range(1, slivers):
        for step in range(steps):
            before = left[step, far - 1]
            below = lax.ppermute(before[0], "rep", up_pairs(far))
            above = lax.ppermute(before[-1], "rep", down_pairs(far))
            left[step, far] = (below, above)

    right = [panel.reshape(-1, tile, tile) for panel in right_panels(own)]

    total = None
    for far in range(slivers):
        for step in range(steps):
            here = jnp.abs(away[step]) == far
            number = spot[step] + jnp.where(away[step] > 0, per, 0)
            stage = jnp.stack(
                [
                    jnp.where(here, number, 0),
                    lists[step, 1],
                    jnp.where(here, lists[step, 2], NC),
                ]
            )
            total = contract(stage, left[step, far], right[step], total)
    return total[None, None]


def solution(mesh):
    return jax.shard_map(
        per_device,
        mesh=mesh,
        in_specs=(P("blk", "rep", None, None, None, None), P("blk", "rep", None, None, None)),
        out_specs=P("blk", "rep", None, None, None),
        check_vma=False,
    )
```

```python
import functools

import jax
import jax.numpy as jnp
from jax import lax
from jax.experimental import pallas as pl
from jax.experimental.pallas import tpu as pltpu
from jax.sharding import PartitionSpec as P

NC = 16
UNROLL = 4


def split(value):
    high = value.astype(jnp.bfloat16)
    low = (value - high.astype(jnp.float32)).astype(jnp.bfloat16)
    return high, low


def contract_kernel(n_left, n_right, first, tasks_ref, *refs):
    left_refs, right_refs = refs[:n_left], refs[n_left : n_left + n_right]
    rest = refs[n_left + n_right :]
    if first:
        out_ref, left_split, total, live = rest
    else:
        before_ref, out_ref, left_split, total, live = rest
    tile = right_refs[0].shape[-1]
    slots = tasks_ref.shape[-1]

    if first:
        total[...] = jnp.zeros_like(total)
    else:
        total[:NC] = before_ref[...]

    base = 0
    for ref in left_refs:
        for s in range(ref.shape[0]):
            for t in range(ref.shape[1]):
                high, low = split(ref[s, t])
                left_split[base, :, :tile] = high
                left_split[base, :, tile:] = low
                base += 1

    for s, right_ref in enumerate(right_refs):
        def pack(j, count):
            live[count] = j
            return count + jnp.where(tasks_ref[s, 2, j] < NC, 1, 0)

        count = lax.fori_loop(0, slots, pack, 0)
        for extra in range(UNROLL):
            live[count + extra] = slots

        def some(i, carry):
            products, targets = [], []
            for u in range(UNROLL):
                j = live[i * UNROLL + u]
                dead = j >= slots
                at = jnp.where(dead, 0, j)
                high, low = split(right_ref[tasks_ref[s, 1, at]])
                both = jnp.concatenate(
                    [
                        jnp.concatenate([high, low], axis=1),
                        jnp.concatenate([high, jnp.zeros_like(low)], axis=1),
                    ],
                    axis=0,
                )
                wide = jnp.dot(
                    left_split[tasks_ref[s, 0, at]], both, preferred_element_type=jnp.float32
                )
                products.append(wide[:, :tile] + wide[:, tile:])
                targets.append(jnp.where(dead, NC, tasks_ref[s, 2, at]))
            for product, target in zip(products, targets):
                total[target] += product
            return carry

        lax.fori_loop(0, (count + UNROLL - 1) // UNROLL, some, 0)
    out_ref[...] = total[:NC]


def contract(tasks, lefts, rights, before):
    tile = rights[0].shape[-1]
    n_tiles = sum(left.shape[0] * left.shape[1] for left in lefts)
    steps, _, slots = tasks.shape
    vmem = pl.BlockSpec(memory_space=pltpu.VMEM)
    operands = [tasks, *lefts, *rights] + ([] if before is None else [before])
    return pl.pallas_call(
        functools.partial(contract_kernel, len(lefts), len(rights), before is None),
        out_shape=jax.ShapeDtypeStruct((NC, tile, tile), jnp.float32),
        in_specs=[pl.BlockSpec(memory_space=pltpu.SMEM)] + [vmem] * (len(operands) - 1),
        out_specs=vmem,
        scratch_shapes=[
            pltpu.VMEM((n_tiles, tile, 2 * tile), jnp.bfloat16),
            pltpu.VMEM((NC + 1, tile, tile), jnp.float32),
            pltpu.SMEM((slots + UNROLL,), jnp.int32),
        ],
        compiler_params=pltpu.CompilerParams(vmem_limit_bytes=24 * 2**20),
        cost_estimate=pl.CostEstimate(
            flops=1150 * 10**6 * steps,
            bytes_accessed=4 * tile * tile * 2 * NC,
            transcendentals=0,
        ),
    )(*operands)


def shift_pairs(count, by):
    return [(i, (i + by) % count) for i in range(count)]


def right_panels(own):
    panels, steps = lax.axis_size("blk"), own.shape[0]
    if steps != 4 or panels % 2:
        found = [own]
        for step in range(1, steps):
            found.append(lax.ppermute(own, "blk", shift_pairs(panels, step)))
        return found
    odd = lax.axis_index("blk") % 2 == 1
    two = lax.ppermute(own, "blk", shift_pairs(panels, 2))
    one = lax.ppermute(
        jnp.where(odd, two, own), "blk", [(i, i ^ 1) for i in range(panels)]
    )
    three = lax.ppermute(
        jnp.where(odd, own, two),
        "blk",
        [(i, (i + 3) % panels if i % 2 else i + 1) for i in range(panels)],
    )
    return [own, one, two, three]


def gathered(own):
    slivers = lax.axis_size("rep")
    me = lax.axis_index("rep")
    if slivers != 4:
        whole = lax.all_gather(own, "rep", axis=0)
        return [([i], (whole[i],)) for i in range(slivers)]
    outer = [(0, 1), (1, 0), (2, 3), (3, 2)]
    inner = [(1, 2), (2, 1)]
    ends = [(1, 0), (2, 3)]
    side = lax.ppermute(own, "rep", outer)
    near = lax.ppermute(own, "rep", inner)
    far = lax.ppermute(side, "rep", inner)
    near_end = lax.ppermute(near, "rep", ends)
    far_end = lax.ppermute(far, "rep", ends)
    low = me < 2
    middle = (me == 1) | (me == 2)
    pick = lambda number: jnp.where(middle, number, -1), lambda number: jnp.where(middle, -1, number)
    inner_of_other, outer_of_other = jnp.where(low, 2, 1), jnp.where(low, 3, 0)
    return [
        ([me], (own,)),
        ([me ^ 1], (side,)),
        ([pick[0](inner_of_other), pick[1](inner_of_other)], (near, near_end)),
        ([pick[0](outer_of_other), pick[1](outer_of_other)], (far, far_end)),
    ]


def per_device(p_tiles, tasks):
    own = p_tiles[0, 0]
    lists = tasks[0, 0]
    steps, per, tile = own.shape[0], own.shape[1], own.shape[-1]
    right = [panel.reshape(-1, tile, tile) for panel in right_panels(own)]
    sliver, spot = lists[:, 0] // per, lists[:, 0] % per
    spot = spot + per * jnp.arange(steps, dtype=spot.dtype)[:, None]

    total = None
    for numbers, lefts in gathered(own):
        here, place = False, 0
        for i, number in enumerate(numbers):
            this = sliver == number
            here = here | this
            place = place + jnp.where(this, spot + i * steps * per, 0)
        stage = jnp.stack([place, lists[:, 1], jnp.where(here, lists[:, 2], NC)], axis=1)
        total = contract(stage, lefts, right, total)
    return total[None, None]


def solution(mesh):
    return jax.shard_map(
        per_device,
        mesh=mesh,
        in_specs=(P("blk", "rep", None, None, None, None), P("blk", "rep", None, None, None)),
        out_specs=P("blk", "rep", None, None, None),
        check_vma=False,
    )
```

```python
import functools

import jax
import jax.numpy as jnp
from jax import lax
from jax.experimental import pallas as pl
from jax.experimental.pallas import tpu as pltpu
from jax.sharding import PartitionSpec as P

NC = 16
UNROLL = 8
LA, LB, LC = 30, 30, 30
VMEM = pl.BlockSpec(memory_space=pltpu.VMEM)
SMEM = pl.BlockSpec(memory_space=pltpu.SMEM)


def split(value):
    high = value.astype(jnp.bfloat16)
    low = (value - high.astype(jnp.float32)).astype(jnp.bfloat16)
    return high, low


def pack(words, keep, spare):
    slots = words.shape[-1]
    number = jnp.arange(slots + UNROLL)
    before = number[:slots, None] > number[None, :slots]
    rank = jnp.sum(keep[..., None, :] & before, axis=-1)
    count = jnp.sum(keep.astype(jnp.int32), axis=-1)
    chosen = keep[..., None, :] & (rank[..., None, :] == number[:, None])
    packed = jnp.sum(jnp.where(chosen, words[..., None, :] - spare, 0), axis=-1) + spare
    return packed, count


def contract_kernel(n_left, n_right, words_ref, counts_ref, *refs):
    left_refs, right_refs = refs[:n_left], refs[n_left : n_left + n_right]
    *before_ref, out_ref, left_split, total = refs[n_left + n_right :]
    tile = right_refs[0].shape[-1]

    some_live = counts_ref[0]
    for p in range(1, n_right):
        some_live = some_live + counts_ref[p]

    @pl.when(some_live > 0)
    def _():
        total[:NC] = before_ref[0][...] if before_ref else jnp.zeros_like(total[:NC])
        base = 0
        for ref in left_refs:
            for s in range(ref.shape[0]):

                def one(t, carry, ref=ref, s=s, base=base):
                    high, low = split(ref[s, t])
                    left_split[base + t, :, :tile] = high
                    left_split[base + t, :, tile:] = low
                    return carry

                lax.fori_loop(0, ref.shape[1], one, 0, unroll=True)
                base += ref.shape[1]

        for p, right_ref in enumerate(right_refs):

            def some(i, carry, p=p, right_ref=right_ref):
                products, targets = [], []
                for u in range(UNROLL):
                    word = words_ref[p, i * UNROLL + u]
                    high, low = split(right_ref[(word >> 8) & 255])
                    both = jnp.concatenate(
                        [
                            jnp.concatenate([high, low], axis=1),
                            jnp.concatenate([high, jnp.zeros_like(low)], axis=1),
                        ],
                        axis=0,
                    )
                    wide = jnp.dot(
                        left_split[word & 255], both, preferred_element_type=jnp.float32
                    )
                    products.append(wide[:, :tile] + wide[:, tile:])
                    targets.append(word >> 16)
                for product, target in zip(products, targets):
                    total[target] += product
                return carry

            lax.fori_loop(0, (counts_ref[p] + UNROLL - 1) // UNROLL, some, 0)
        out_ref[...] = total[:NC]

    @pl.when(some_live == 0)
    def _():
        out_ref[...] = before_ref[0][...] if before_ref else jnp.zeros_like(out_ref)


def contract(planned, lefts, rights, before=None, token=None):
    tile = rights[0].shape[-1]
    n_tiles = sum(left.shape[0] * left.shape[1] for left in lefts)
    if token is not None:
        planned, _ = lax.optimization_barrier((planned, token))
    operands = [*planned, *lefts, *rights] + ([] if before is None else [before])
    return pl.pallas_call(
        functools.partial(contract_kernel, len(lefts), len(rights)),
        out_shape=jax.ShapeDtypeStruct((NC, tile, tile), jnp.float32),
        in_specs=[SMEM] * 2 + [VMEM] * (len(operands) - 2),
        out_specs=VMEM,
        scratch_shapes=[
            pltpu.VMEM((n_tiles, tile, 2 * tile), jnp.bfloat16),
            pltpu.VMEM((NC + 1, tile, tile), jnp.float32),
        ],
        compiler_params=pltpu.CompilerParams(vmem_limit_bytes=24 * 2**20),
        cost_estimate=pl.CostEstimate(flops=1000, bytes_accessed=1000, transcendentals=0),
    )(*operands)


def later(seed, value, cost):
    seed, _ = lax.optimization_barrier((seed, value))

    def kernel(seed_ref, out_ref):
        out_ref[0] = seed_ref[0]

    return pl.pallas_call(
        kernel,
        out_shape=jax.ShapeDtypeStruct((1,), jnp.int32),
        in_specs=[SMEM],
        out_specs=SMEM,
        cost_estimate=pl.CostEstimate(flops=cost * 1150 * 10**6, bytes_accessed=0, transcendentals=0),
    )(seed)


def ring(count, by):
    return [(i, (i + by) % count) for i in range(count)]


def general(own, lists):
    steps, per, tile = own.shape[0], own.shape[1], own.shape[-1]
    panels, slivers = lax.axis_size("blk"), lax.axis_size("rep")
    whole = lax.all_gather(own, "rep", axis=0)
    total = None
    for step in range(steps):
        right = lax.ppermute(own, "blk", ring(panels, step)) if step else own
        left = whole[:, step]
        used = lists[step, 2] < NC
        word = lists[step, 0] | (lists[step, 1] << 8) | (lists[step, 2] << 16)
        total = contract(pack(word[None], used[None], NC << 16), [left], [right.reshape(-1, tile, tile)], total)
    return total


def helped(own, lists):
    steps, per, tile = own.shape[0], own.shape[1], own.shape[-1]
    panels, slivers = lax.axis_size("blk"), lax.axis_size("rep")
    blk, rep = lax.axis_index("blk"), lax.axis_index("rep")
    even, odd = range(0, panels, 2), range(1, panels, 2)
    every = range(panels)
    inward, outward, across = [(0, 1), (3, 2)], [(1, 0), (2, 3)], [(1, 2), (2, 1)]

    def send(value, *routes):
        pairs = [
            (b * slivers + source, (b + on) % panels * slivers + target)
            for these, ways, on in routes
            for b in these
            for source, target in ways
        ]
        return lax.ppermute(value, ("blk", "rep"), pairs)

    here = [(i, i) for i in range(slivers)]
    middle = [(1, 1), (2, 2)]
    flat = lambda x: x.reshape(-1, tile, tile)

    beyond = [(0, 2), (3, 1)]
    after = lambda value, *tokens: lax.optimization_barrier((value, *tokens))[0]

    side = send(own, (every, inward, 0), (even, outward, 0))
    near = send(own, (every, across, 0))
    two = send(own, (every, here, 2))
    their_lists = send(lists, (odd, inward, 0))
    side, near = lax.optimization_barrier((side, near))
    seed = jnp.zeros((1,), jnp.int32) + rep.astype(jnp.int32)

    far_even = send(side, (even, across, 0))
    near_end = send(near, (even, outward, 0))
    swapped = send(two, (even, here, 1), (odd, here, -1))
    theirs_two = send(side, (odd, middle, 2))
    theirs = [side, send(side, (even, middle, 1)), theirs_two, send(two, (even, inward, 1))]
    token = later(seed, (far_even, near_end), LA)
    alternate = send(after(own, theirs_two, token), (even, here, 1), (odd, here, 3))
    far_odd = send(after(side, theirs_two, token), (odd, across, 0))
    far_end = send(far_even, (even, outward, 0))
    late = later(seed, far_end, LC)

    is_odd = blk % 2 == 1
    is_middle = (rep == 1) | (rep == 2)
    block = steps * per

    def words(these, sliver_is, first):
        left = these[:, 0] % per + per * jnp.arange(steps)[:, None]
        for is_it, begin in zip(sliver_is, first):
            left = left + jnp.where(is_it, begin, 0)
        return left | (these[:, 1] << 8) | (these[:, 2] << 16)

    def slivers_of(these):
        sliver = these[:, 0] // per
        inner, outer = jnp.where(rep < 2, 2, 1), jnp.where(rep < 2, 3, 0)
        return [sliver == i for i in (rep, rep ^ 1, inner, outer)]

    def by_panel(these):
        return jnp.where(is_odd, these, jnp.stack([these[i] for i in (0, 3, 2, 1)]))

    spare = NC << 16
    live = lists[:, 2] < NC
    mine, beside, inner, outer = which = slivers_of(lists)
    full = is_middle | ~is_odd
    begin = jnp.where(is_middle, jnp.where(is_odd, 2 * block, block), 0)
    word = words(lists, which, [0, block, jnp.where(is_middle, 2 * block, 3 * block), begin])
    use_one = live & (mine | (full & (beside | inner)))
    use_two = live & outer & full
    mine, beside, inner, outer = which = slivers_of(their_lists)
    help_word = words(their_lists, which, [0, 0, block, 0])
    helping = (their_lists[:, 2] < NC) & is_middle & is_odd
    use_help = [helping & (mine | inner), helping & outer]

    panels_of = [flat(x) for x in theirs]
    part = contract(pack(help_word, use_help[0], spare), [own, near], panels_of)
    part = contract(pack(help_word, use_help[1], spare), [far_odd], panels_of, part)
    part = send(part, (odd, outward, 0))

    rights = [flat(x) for x in (own, alternate, two, swapped)]
    word = by_panel(word)
    total = contract(
        pack(word, by_panel(use_one), spare), [own, side, near, near_end], rights
    )
    total = contract(
        pack(word, by_panel(use_two), spare), [far_end, far_even, far_odd], rights, total, late
    )
    return total + part


def per_device(p_tiles, tasks):
    own, lists = p_tiles[0, 0], tasks[0, 0]
    small = lax.axis_size("rep") == 4 and own.shape[0] == 4 and lax.axis_size("blk") % 2 == 0
    return (helped if small else general)(own, lists)[None, None]


def solution(mesh):
    return jax.shard_map(
        per_device,
        mesh=mesh,
        in_specs=(P("blk", "rep", None, None, None, None), P("blk", "rep", None, None, None)),
        out_specs=P("blk", "rep", None, None, None),
        check_vma=False,
    )
```

```python
import functools

import jax
import jax.numpy as jnp
from jax import lax
from jax.experimental import pallas as pl
from jax.experimental.pallas import tpu as pltpu
from jax.sharding import PartitionSpec as P

NC = 16
UNROLL = 16
VMEM = pl.BlockSpec(memory_space=pltpu.VMEM)
SMEM = pl.BlockSpec(memory_space=pltpu.SMEM)
ANY = pl.BlockSpec(memory_space=pl.ANY)


def split(value):
    high = value.astype(jnp.bfloat16)
    low = (value - high.astype(jnp.float32)).astype(jnp.bfloat16)
    return high, low


def pack(words, keep):
    words, keep = words.reshape(-1), keep.reshape(-1)
    slots = words.shape[0]
    spare = NC << 16
    number = jnp.arange(slots + UNROLL)
    rank = jnp.sum(keep[None, :] & (number[:slots, None] > number[None, :slots]), axis=1)
    count = jnp.sum(keep.astype(jnp.int32), keepdims=True)
    chosen = keep[None, :] & (rank[None, :] == number[:, None])
    packed = jnp.sum(jnp.where(chosen, words[None, :] - spare, 0), axis=1) + spare
    return jnp.concatenate([packed, count])


def contract_kernel(placed, n_left, n_right, words_ref, *refs):
    left_refs, right_refs = refs[:n_left], refs[n_left : n_left + n_right]
    *before_ref, out_ref, left_raw, right_raw, total, sems = refs[n_left + n_right :]
    block, tile = right_refs[0].shape[0], right_refs[0].shape[-1]
    count, kind = (words_ref[words_ref.shape[0] - i] for i in (2, 1))

    @pl.when(count > 0)
    def _():
        blocks = left_raw.shape[0] // block

        def lefts(act):
            for b, places in enumerate(placed):
                for at in sorted(set(places) - {None}):
                    here = functools.reduce(
                        jnp.logical_or, [kind == c for c, place in enumerate(places) if place == at]
                    )
                    copy = pltpu.make_async_copy(
                        left_refs[b], left_raw.at[pl.ds(at * block, block)], sems.at[at]
                    )
                    pl.when(here)(functools.partial(act, copy))

        rights = [
            pltpu.make_async_copy(ref, right_raw.at[pl.ds(k * block, block)], sems.at[blocks + k])
            for k, ref in enumerate(right_refs)
        ]
        lefts(lambda copy: copy.start())
        for copy in rights:
            copy.start()
        total[:NC] = before_ref[0][...] if before_ref else jnp.zeros_like(total[:NC])
        lefts(lambda copy: copy.wait())

        for copy in rights:
            copy.wait()

        def some(i, carry):
            products, targets = [], []
            for u in range(UNROLL):
                word = words_ref[i * UNROLL + u]
                high, low = split(right_raw[(word >> 8) & 255])
                both = jnp.concatenate(
                    [
                        jnp.concatenate([high, low], axis=1),
                        jnp.concatenate([high, jnp.zeros_like(low)], axis=1),
                    ],
                    axis=0,
                )
                pair = jnp.concatenate(split(left_raw[word & 255]), axis=1)
                wide = jnp.dot(pair, both, preferred_element_type=jnp.float32)
                products.append(wide[:, :tile] + wide[:, tile:])
                targets.append(word >> 16)
            for product, target in zip(products, targets):
                total[target] += product
            return carry

        lax.fori_loop(0, (count + UNROLL - 1) // UNROLL, some, 0)
        out_ref[...] = total[:NC]

    @pl.when(count == 0)
    def _():
        out_ref[...] = before_ref[0][...] if before_ref else jnp.zeros_like(out_ref)


def contract(planned, lefts, rights, before=None, placed=None, kind=0):
    block, tile = rights[0].shape[0], rights[0].shape[-1]
    placed = placed or [(b,) for b in range(len(lefts))]
    blocks = 1 + max(place for places in placed for place in places if place is not None)
    planned = jnp.append(planned, jnp.int32(kind))
    lefts, rights = [
        [pltpu.with_memory_space_constraint(x, pltpu.HBM) for x in xs] for xs in (lefts, rights)
    ]
    operands = [planned, *lefts, *rights] + ([] if before is None else [before])
    size = (blocks * block + len(rights) * block + 3 * NC + 1) * tile * tile
    return pl.pallas_call(
        functools.partial(contract_kernel, placed, len(lefts), len(rights)),
        out_shape=pltpu.VMEM((NC, tile, tile), jnp.float32),
        in_specs=[SMEM] + [ANY] * (len(lefts) + len(rights)) + [VMEM] * (before is not None),
        out_specs=VMEM,
        scratch_shapes=[
            pltpu.VMEM((blocks * block, tile, tile), jnp.float32),
            pltpu.VMEM((len(rights) * block, tile, tile), jnp.float32),
            pltpu.VMEM((NC + 1, tile, tile), jnp.float32),
            pltpu.SemaphoreType.DMA((blocks + len(rights),)),
        ],
        compiler_params=pltpu.CompilerParams(vmem_limit_bytes=4 * size + 4 * 2**20),
        cost_estimate=pl.CostEstimate(flops=1000, bytes_accessed=1000, transcendentals=0),
    )(*operands)


def probe(value):
    corner = value[(0,) * (value.ndim - 2) + (slice(0, 1), slice(0, 1))].reshape(1)
    return jnp.minimum(jnp.abs(corner), 0).astype(jnp.int32)


def ring(count, by):
    return [(i, (i + by) % count) for i in range(count)]


def general(own, lists):
    steps, tile = own.shape[0], own.shape[-1]
    panels = lax.axis_size("blk")
    whole = lax.all_gather(own, "rep", axis=0)
    total = None
    for step in range(steps):
        right = lax.ppermute(own, "blk", ring(panels, step)) if step else own
        word = lists[step, 0] | (lists[step, 1] << 8) | (lists[step, 2] << 16)
        total = contract(
            pack(word, lists[step, 2] < NC),
            [whole[:, step].reshape(-1, tile, tile)],
            [right.reshape(-1, tile, tile)],
            total,
        )
    return total


def on_a_line(own, lists):
    steps, per, tile = own.shape[0], own.shape[1], own.shape[-1]
    panels, slivers = lax.axis_size("blk"), lax.axis_size("rep")
    blk, rep = lax.axis_index("blk"), lax.axis_index("rep")
    even, odd, every = range(0, panels, 2), range(1, panels, 2), range(panels)
    inward, outward, across, beyond = [(0, 1), (3, 2)], [(1, 0), (2, 3)], [(1, 2), (2, 1)], [(0, 2), (3, 1)]
    here = [(i, i) for i in range(slivers)]
    middle = [(1, 1), (2, 2)]
    block = steps * per

    def send(value, *routes):
        pairs = [
            (b * slivers + source, (b + on) % panels * slivers + target)
            for these, ways, on in routes
            for b in these
            for source, target in ways
        ]
        return lax.ppermute(value, ("blk", "rep"), pairs)

    is_odd, is_middle = blk % 2 == 1, (rep == 1) | (rep == 2)
    full = is_middle | ~is_odd
    kind = 2 * is_odd.astype(jnp.int32) + 1 - is_middle.astype(jnp.int32)

    sliver = lists[:, 0] // per
    steps_of = jnp.arange(steps)[:, None]
    place = lists[:, 0] % per + per * steps_of + (lists[:, 1] << 8) + (lists[:, 2] << 16)
    live = lists[:, 2] < NC
    mine, beside, inner, outer = [
        sliver == i for i in (rep, rep ^ 1, jnp.where(rep < 2, 2, 1), jnp.where(rep < 2, 3, 0))
    ]

    def words(panel, *firsts):
        word = place + ((panel * block) << 8)
        for is_it, first in zip((mine, beside, inner, outer), firsts):
            word = word + jnp.where(is_it, first, 0)
        return word

    panel = jnp.where(is_odd, steps_of, jnp.array([0, 3, 2, 1])[:, None])
    own_words = pack(words(panel, 0, block, 2 * block, 3 * block), live & (mine | full))
    their_words = pack(words(steps_of, 0, 0, block, 2 * block), live & is_odd & ~is_middle & ~mine)

    p1 = send(own, (even, beyond + outward, 0))
    p2 = send(own, (even, across, 0), (odd, inward, 0))
    p3 = send(own, (even, inward, 0), (odd, across, 0))
    two = send(own, (every, here, 2))
    their_words = send(their_words, (odd, inward, 0))
    alternate = send(own, (even, here, 1), (odd, here, 3))
    q1 = send(p2, (even, outward, 0), (odd, across, 0))
    q2 = send(jnp.where(is_middle, p1, two), (even, outward, 0), (even, inward, 1))
    h2 = send(p2, (odd, middle, 2))
    h1 = send(p3, (even, middle, 1))
    swapped = send(two, (even, here, 1), (odd, here, -1))

    own, p1, p2, p3, q1, q2, h1, h2, two, alternate, swapped = [
        x.reshape(-1, tile, tile) for x in (own, p1, p2, p3, q1, q2, h1, h2, two, alternate, swapped)
    ]
    part = contract(their_words + probe(alternate), [own, p3, q1], [p2, h1, h2, q2])
    part = send(part, (odd, outward, 0))

    lefts = [own, p1, p2, p3, q1, q2]
    placed = [
        (0, 0, 0, 0),
        (3, 1, None, None),
        (2, None, 1, None),
        (1, None, 2, None),
        (None, 2, 3, None),
        (None, 3, None, None),
    ]
    total = contract(own_words, lefts, [own, alternate, two, swapped], None, placed, kind)
    return total + part


def per_device(p_tiles, tasks):
    own, lists = p_tiles[0, 0], tasks[0, 0]
    small = lax.axis_size("rep") == 4 and own.shape[0] == 4 and lax.axis_size("blk") % 2 == 0
    return (on_a_line if small else general)(own, lists)[None, None]


def solution(mesh):
    return jax.shard_map(
        per_device,
        mesh=mesh,
        in_specs=(P("blk", "rep", None, None, None, None), P("blk", "rep", None, None, None)),
        out_specs=P("blk", "rep", None, None, None),
        check_vma=False,
    )
```

```python
import functools

import jax
import jax.numpy as jnp
from jax import lax
from jax.experimental import pallas as pl
from jax.experimental.pallas import tpu as pltpu
from jax.sharding import PartitionSpec as P

NC = 16
UNROLL = 16
VMEM = pl.BlockSpec(memory_space=pltpu.VMEM)
SMEM = pl.BlockSpec(memory_space=pltpu.SMEM)
ANY = pl.BlockSpec(memory_space=pl.ANY)


def split(value):
    high = value.astype(jnp.bfloat16)
    low = (value - high.astype(jnp.float32)).astype(jnp.bfloat16)
    return high, low


def pack(words, keep):
    words, keep = words.reshape(-1), keep.reshape(-1)
    slots = words.shape[0]
    spare = NC << 16
    number = jnp.arange(slots + UNROLL)
    rank = jnp.sum(keep[None, :] & (number[:slots, None] > number[None, :slots]), axis=1)
    count = jnp.sum(keep.astype(jnp.int32), keepdims=True)
    chosen = keep[None, :] & (rank[None, :] == number[:, None])
    packed = jnp.sum(jnp.where(chosen, words[None, :] - spare, 0), axis=1) + spare
    return jnp.concatenate([packed, count])


def contract_kernel(placed, n_left, n_right, words_ref, *refs):
    left_refs, right_refs = refs[:n_left], refs[n_left : n_left + n_right]
    *before_ref, out_ref, left_raw, right_raw, total, sems = refs[n_left + n_right :]
    block, tile = right_refs[0].shape[0], right_refs[0].shape[-1]
    count, kind = (words_ref[words_ref.shape[0] - i] for i in (2, 1))

    @pl.when(count > 0)
    def _():
        blocks = left_raw.shape[0] // block

        def lefts(act):
            for b, places in enumerate(placed):
                for at in sorted(set(places) - {None}):
                    here = functools.reduce(
                        jnp.logical_or, [kind == c for c, place in enumerate(places) if place == at]
                    )
                    copy = pltpu.make_async_copy(
                        left_refs[b], left_raw.at[pl.ds(at * block, block)], sems.at[at]
                    )
                    pl.when(here)(functools.partial(act, copy))

        rights = [
            pltpu.make_async_copy(ref, right_raw.at[pl.ds(k * block, block)], sems.at[blocks + k])
            for k, ref in enumerate(right_refs)
        ]
        lefts(lambda copy: copy.start())
        for copy in rights:
            copy.start()
        total[:NC] = before_ref[0][...] if before_ref else jnp.zeros_like(total[:NC])
        lefts(lambda copy: copy.wait())


        def some(i, ready):
            numbers = [words_ref[i * UNROLL + u] for u in range(UNROLL)]
            most = functools.reduce(jnp.maximum, [(word >> 8) & 255 for word in numbers])
            for k, copy in enumerate(rights):
                pl.when((ready <= k) & (most >= k * block))(copy.wait)
            products, targets = [], []
            for word in numbers:
                high, low = split(right_raw[(word >> 8) & 255])
                both = jnp.concatenate(
                    [
                        jnp.concatenate([high, low], axis=1),
                        jnp.concatenate([high, jnp.zeros_like(low)], axis=1),
                    ],
                    axis=0,
                )
                pair = jnp.concatenate(split(left_raw[word & 255]), axis=1)
                wide = jnp.dot(pair, both, preferred_element_type=jnp.float32)
                products.append(wide[:, :tile] + wide[:, tile:])
                targets.append(word >> 16)
            for product, target in zip(products, targets):
                total[target] += product
            return jnp.maximum(ready, sum(jnp.where(most >= k * block, 1, 0) for k in range(n_right)))

        ready = lax.fori_loop(0, (count + UNROLL - 1) // UNROLL, some, 0)
        for k, copy in enumerate(rights):
            pl.when(ready <= k)(copy.wait)
        out_ref[...] = total[:NC]

    @pl.when(count == 0)
    def _():
        out_ref[...] = before_ref[0][...] if before_ref else jnp.zeros_like(out_ref)


def contract(planned, lefts, rights, before=None, placed=None, kind=0):
    block, tile = rights[0].shape[0], rights[0].shape[-1]
    placed = placed or [(b,) for b in range(len(lefts))]
    blocks = 1 + max(place for places in placed for place in places if place is not None)
    planned = jnp.append(planned, jnp.int32(kind))
    lefts, rights = [
        [pltpu.with_memory_space_constraint(x, pltpu.HBM) for x in xs] for xs in (lefts, rights)
    ]
    operands = [planned, *lefts, *rights] + ([] if before is None else [before])
    size = (blocks * block + len(rights) * block + 3 * NC + 1) * tile * tile
    return pl.pallas_call(
        functools.partial(contract_kernel, placed, len(lefts), len(rights)),
        out_shape=pltpu.VMEM((NC, tile, tile), jnp.float32),
        in_specs=[SMEM] + [ANY] * (len(lefts) + len(rights)) + [VMEM] * (before is not None),
        out_specs=VMEM,
        scratch_shapes=[
            pltpu.VMEM((blocks * block, tile, tile), jnp.float32),
            pltpu.VMEM((len(rights) * block, tile, tile), jnp.float32),
            pltpu.VMEM((NC + 1, tile, tile), jnp.float32),
            pltpu.SemaphoreType.DMA((blocks + len(rights),)),
        ],
        compiler_params=pltpu.CompilerParams(vmem_limit_bytes=4 * size + 4 * 2**20),
        cost_estimate=pl.CostEstimate(flops=1000, bytes_accessed=1000, transcendentals=0),
    )(*operands)


def probe(value):
    corner = value[(0,) * (value.ndim - 2) + (slice(0, 1), slice(0, 1))].reshape(1)
    return jnp.minimum(jnp.abs(corner), 0).astype(jnp.int32)


def ring(count, by):
    return [(i, (i + by) % count) for i in range(count)]


def general(own, lists):
    steps, tile = own.shape[0], own.shape[-1]
    panels = lax.axis_size("blk")
    whole = lax.all_gather(own, "rep", axis=0)
    total = None
    for step in range(steps):
        right = lax.ppermute(own, "blk", ring(panels, step)) if step else own
        word = lists[step, 0] | (lists[step, 1] << 8) | (lists[step, 2] << 16)
        total = contract(
            pack(word, lists[step, 2] < NC),
            [whole[:, step].reshape(-1, tile, tile)],
            [right.reshape(-1, tile, tile)],
            total,
        )
    return total


def on_a_line(own, lists):
    steps, per, tile = own.shape[0], own.shape[1], own.shape[-1]
    panels, slivers = lax.axis_size("blk"), lax.axis_size("rep")
    blk, rep = lax.axis_index("blk"), lax.axis_index("rep")
    even, odd, every = range(0, panels, 2), range(1, panels, 2), range(panels)
    inward, outward, across, beyond = [(0, 1), (3, 2)], [(1, 0), (2, 3)], [(1, 2), (2, 1)], [(0, 2), (3, 1)]
    here = [(i, i) for i in range(slivers)]
    middle = [(1, 1), (2, 2)]
    block = steps * per

    def send(value, *routes):
        pairs = [
            (b * slivers + source, (b + on) % panels * slivers + target)
            for these, ways, on in routes
            for b in these
            for source, target in ways
        ]
        return lax.ppermute(value, ("blk", "rep"), pairs)

    is_odd, is_middle = blk % 2 == 1, (rep == 1) | (rep == 2)
    full = is_middle | ~is_odd
    kind = 2 * is_odd.astype(jnp.int32) + 1 - is_middle.astype(jnp.int32)

    sliver = lists[:, 0] // per
    steps_of = jnp.arange(steps)[:, None]
    place = lists[:, 0] % per + per * steps_of + (lists[:, 1] << 8) + (lists[:, 2] << 16)
    live = lists[:, 2] < NC
    mine, beside, inner, outer = [
        sliver == i for i in (rep, rep ^ 1, jnp.where(rep < 2, 2, 1), jnp.where(rep < 2, 3, 0))
    ]

    def words(panel, *firsts):
        word = place + ((panel * block) << 8)
        for is_it, first in zip((mine, beside, inner, outer), firsts):
            word = word + jnp.where(is_it, first, 0)
        return word

    panel = jnp.where(is_odd, steps_of, jnp.array([0, 3, 2, 1])[:, None])
    own_words = pack(words(panel, 0, block, 2 * block, 3 * block), live & (mine | full))
    their_words = pack(words(steps_of, 0, 0, block, 2 * block), live & is_odd & ~is_middle & ~mine)

    p1 = send(own, (even, beyond + outward, 0))
    p2 = send(own, (even, across, 0), (odd, inward, 0))
    p3 = send(own, (even, inward, 0), (odd, across, 0))
    two = send(own, (every, here, 2))
    their_words = send(their_words, (odd, inward, 0))
    alternate = send(own, (even, here, 1), (odd, here, 3))
    q1 = send(p2, (even, outward, 0), (odd, across, 0))
    q2 = send(jnp.where(is_middle, p1, two), (even, outward, 0), (even, inward, 1))
    h2 = send(p2, (odd, middle, 2))
    h1 = send(p3, (even, middle, 1))
    swapped = send(two, (even, here, 1), (odd, here, -1))

    own, p1, p2, p3, q1, q2, h1, h2, two, alternate, swapped = [
        x.reshape(-1, tile, tile) for x in (own, p1, p2, p3, q1, q2, h1, h2, two, alternate, swapped)
    ]
    part = contract(their_words + probe(alternate), [own, p3, q1], [p2, h1, h2, q2])
    part = send(part, (odd, outward, 0))

    lefts = [own, p1, p2, p3, q1, q2]
    placed = [
        (0, 0, 0, 0),
        (3, 1, None, None),
        (2, None, 1, None),
        (1, None, 2, None),
        (None, 2, 3, None),
        (None, 3, None, None),
    ]
    total = contract(own_words, lefts, [own, alternate, two, swapped], None, placed, kind)
    return total + part


def per_device(p_tiles, tasks):
    own, lists = p_tiles[0, 0], tasks[0, 0]
    small = lax.axis_size("rep") == 4 and own.shape[0] == 4 and lax.axis_size("blk") % 2 == 0
    return (on_a_line if small else general)(own, lists)[None, None]


def solution(mesh):
    return jax.shard_map(
        per_device,
        mesh=mesh,
        in_specs=(P("blk", "rep", None, None, None, None), P("blk", "rep", None, None, None)),
        out_specs=P("blk", "rep", None, None, None),
        check_vma=False,
    )
```

```python
import functools

import jax
import jax.numpy as jnp
from jax import lax
from jax.experimental import pallas as pl
from jax.experimental.pallas import tpu as pltpu
from jax.sharding import PartitionSpec as P

NC = 16
UNROLL = 16
VMEM = pl.BlockSpec(memory_space=pltpu.VMEM)
SMEM = pl.BlockSpec(memory_space=pltpu.SMEM)
ANY = pl.BlockSpec(memory_space=pl.ANY)


def split(value):
    high = value.astype(jnp.bfloat16)
    low = (value - high.astype(jnp.float32)).astype(jnp.bfloat16)
    return high, low


def pack(words, keep):
    words, keep = words.reshape(-1), keep.reshape(-1)
    slots = words.shape[0]
    spare = NC << 16
    number = jnp.arange(slots + UNROLL)
    rank = jnp.sum(keep[None, :] & (number[:slots, None] > number[None, :slots]), axis=1)
    count = jnp.sum(keep.astype(jnp.int32), keepdims=True)
    chosen = keep[None, :] & (rank[None, :] == number[:, None])
    packed = jnp.sum(jnp.where(chosen, words[None, :] - spare, 0), axis=1) + spare
    return jnp.concatenate([packed, count])


def contract_kernel(placed, n_left, n_right, words_ref, *refs):
    left_refs, right_refs = refs[:n_left], refs[n_left : n_left + n_right]
    *before_ref, out_ref, left_raw, right_raw, total, sems = refs[n_left + n_right :]
    block, tile = right_refs[0].shape[0], right_refs[0].shape[-1]
    count, kind = (words_ref[words_ref.shape[0] - i] for i in (2, 1))

    @pl.when(count > 0)
    def _():
        blocks = left_raw.shape[0] // block

        def lefts(act):
            for b, places in enumerate(placed):
                for at in sorted(set(places) - {None}):
                    here = functools.reduce(
                        jnp.logical_or, [kind == c for c, place in enumerate(places) if place == at]
                    )
                    copy = pltpu.make_async_copy(
                        left_refs[b], left_raw.at[pl.ds(at * block, block)], sems.at[at]
                    )
                    pl.when(here)(functools.partial(act, copy))

        rights = [
            pltpu.make_async_copy(ref, right_raw.at[pl.ds(k * block, block)], sems.at[blocks + k])
            for k, ref in enumerate(right_refs)
        ]
        lefts(lambda copy: copy.start())
        for copy in rights:
            copy.start()
        total[:NC] = before_ref[0][...] if before_ref else jnp.zeros_like(total[:NC])
        lefts(lambda copy: copy.wait())


        def some(i, ready):
            numbers = [words_ref[i * UNROLL + u] for u in range(UNROLL)]
            most = functools.reduce(jnp.maximum, [(word >> 8) & 255 for word in numbers])
            for k, copy in enumerate(rights):
                pl.when((ready <= k) & (most >= k * block))(copy.wait)
            products, targets = [], []
            for word in numbers:
                high, low = split(right_raw[(word >> 8) & 255])
                both = jnp.concatenate(
                    [
                        jnp.concatenate([high, low], axis=1),
                        jnp.concatenate([high, jnp.zeros_like(low)], axis=1),
                    ],
                    axis=0,
                )
                pair = jnp.concatenate(split(left_raw[word & 255]), axis=1)
                wide = jnp.dot(pair, both, preferred_element_type=jnp.float32)
                products.append(wide[:, :tile] + wide[:, tile:])
                targets.append(word >> 16)
            for product, target in zip(products, targets):
                total[target] += product
            return jnp.maximum(ready, sum(jnp.where(most >= k * block, 1, 0) for k in range(n_right)))

        ready = lax.fori_loop(0, (count + UNROLL - 1) // UNROLL, some, 0)
        for k, copy in enumerate(rights):
            pl.when(ready <= k)(copy.wait)
        out_ref[...] = total[:NC]

    @pl.when(count == 0)
    def _():
        out_ref[...] = before_ref[0][...] if before_ref else jnp.zeros_like(out_ref)


def contract(planned, lefts, rights, before=None, placed=None, kind=0):
    block, tile = rights[0].shape[0], rights[0].shape[-1]
    placed = placed or [(b,) for b in range(len(lefts))]
    blocks = 1 + max(place for places in placed for place in places if place is not None)
    planned = jnp.append(planned, jnp.int32(kind))
    operands = [planned, *lefts, *rights] + ([] if before is None else [before])
    size = (blocks * block + len(rights) * block + 3 * NC + 1) * tile * tile
    return pl.pallas_call(
        functools.partial(contract_kernel, placed, len(lefts), len(rights)),
        out_shape=pltpu.VMEM((NC, tile, tile), jnp.float32),
        in_specs=[SMEM] + [ANY] * (len(lefts) + len(rights)) + [VMEM] * (before is not None),
        out_specs=VMEM,
        scratch_shapes=[
            pltpu.VMEM((blocks * block, tile, tile), jnp.float32),
            pltpu.VMEM((len(rights) * block, tile, tile), jnp.float32),
            pltpu.VMEM((NC + 1, tile, tile), jnp.float32),
            pltpu.SemaphoreType.DMA((blocks + len(rights),)),
        ],
        compiler_params=pltpu.CompilerParams(vmem_limit_bytes=4 * size + 4 * 2**20),
        cost_estimate=pl.CostEstimate(flops=1000, bytes_accessed=1000, transcendentals=0),
    )(*operands)


def probe(value):
    corner = value[(0,) * (value.ndim - 2) + (slice(0, 1), slice(0, 1))].reshape(1)
    return jnp.minimum(jnp.abs(corner), 0).astype(jnp.int32)


def ring(count, by):
    return [(i, (i + by) % count) for i in range(count)]


def general(own, lists):
    steps, tile = own.shape[0], own.shape[-1]
    panels = lax.axis_size("blk")
    whole = lax.all_gather(own, "rep", axis=0)
    total = None
    for step in range(steps):
        right = lax.ppermute(own, "blk", ring(panels, step)) if step else own
        word = lists[step, 0] | (lists[step, 1] << 8) | (lists[step, 2] << 16)
        total = contract(
            pack(word, lists[step, 2] < NC),
            [whole[:, step].reshape(-1, tile, tile)],
            [right.reshape(-1, tile, tile)],
            total,
        )
    return total


def on_a_line(own, lists):
    steps, per, tile = own.shape[0], own.shape[1], own.shape[-1]
    panels, slivers = lax.axis_size("blk"), lax.axis_size("rep")
    blk, rep = lax.axis_index("blk"), lax.axis_index("rep")
    even, odd, every = range(0, panels, 2), range(1, panels, 2), range(panels)
    inward, outward, across, beyond = [(0, 1), (3, 2)], [(1, 0), (2, 3)], [(1, 2), (2, 1)], [(0, 2), (3, 1)]
    here = [(i, i) for i in range(slivers)]
    middle = [(1, 1), (2, 2)]
    block = steps * per

    def send(value, *routes):
        pairs = [
            (b * slivers + source, (b + on) % panels * slivers + target)
            for these, ways, on in routes
            for b in these
            for source, target in ways
        ]
        return lax.ppermute(value, ("blk", "rep"), pairs)

    is_odd, is_middle = blk % 2 == 1, (rep == 1) | (rep == 2)
    full = is_middle | ~is_odd
    kind = 2 * is_odd.astype(jnp.int32) + 1 - is_middle.astype(jnp.int32)

    sliver = lists[:, 0] // per
    steps_of = jnp.arange(steps)[:, None]
    place = lists[:, 0] % per + per * steps_of + (lists[:, 1] << 8) + (lists[:, 2] << 16)
    live = lists[:, 2] < NC
    mine, beside, inner, outer = [
        sliver == i for i in (rep, rep ^ 1, jnp.where(rep < 2, 2, 1), jnp.where(rep < 2, 3, 0))
    ]

    def words(panel, *firsts):
        word = place + ((panel * block) << 8)
        for is_it, first in zip((mine, beside, inner, outer), firsts):
            word = word + jnp.where(is_it, first, 0)
        return word

    panel = jnp.where(is_odd, steps_of, jnp.array([0, 3, 2, 1])[:, None])
    own_words = pack(words(panel, 0, block, 2 * block, 3 * block), live & (mine | full))
    their_words = pack(words(steps_of, 0, 0, block, 2 * block), live & is_odd & ~is_middle & ~mine)

    p1 = send(own, (even, beyond + outward, 0))
    p2 = send(own, (even, across, 0), (odd, inward, 0))
    p3 = send(own, (even, inward, 0), (odd, across, 0))
    two = send(own, (every, here, 2))
    their_words = send(their_words, (odd, inward, 0))
    alternate = send(own, (even, here, 1), (odd, here, 3))
    q1 = send(p2, (even, outward, 0), (odd, across, 0))
    q2 = send(jnp.where(is_middle, p1, two), (even, outward, 0), (even, inward, 1))
    h2 = send(p2, (odd, middle, 2))
    h1 = send(p3, (even, middle, 1))
    swapped = send(two, (even, here, 1), (odd, here, -1))

    own, p1, p2, p3, q1, q2, h1, h2, two, alternate, swapped = [
        x.reshape(-1, tile, tile) for x in (own, p1, p2, p3, q1, q2, h1, h2, two, alternate, swapped)
    ]
    their_words = their_words + probe(alternate)
    own, p1, p2, p3, two, q2, swapped, alternate = [
        pltpu.with_memory_space_constraint(x, pltpu.HBM)
        for x in (own, p1, p2, p3, two, q2, swapped, alternate)
    ]
    part = contract(their_words, [own, p3, q1], [p2, h1, h2, q2])
    part = send(part, (odd, outward, 0))

    lefts = [own, p1, p2, p3, q1, q2]
    placed = [
        (0, 0, 0, 0),
        (3, 1, None, None),
        (2, None, 1, None),
        (1, None, 2, None),
        (None, 2, 3, None),
        (None, 3, None, None),
    ]
    total = contract(own_words, lefts, [own, alternate, two, swapped], None, placed, kind)
    return total + part


def per_device(p_tiles, tasks):
    own, lists = p_tiles[0, 0], tasks[0, 0]
    small = lax.axis_size("rep") == 4 and own.shape[0] == 4 and lax.axis_size("blk") % 2 == 0
    return (on_a_line if small else general)(own, lists)[None, None]


def solution(mesh):
    return jax.shard_map(
        per_device,
        mesh=mesh,
        in_specs=(P("blk", "rep", None, None, None, None), P("blk", "rep", None, None, None)),
        out_specs=P("blk", "rep", None, None, None),
        check_vma=False,
    )
```

```python
import functools

import jax
import jax.numpy as jnp
from jax import lax
from jax.experimental import pallas as pl
from jax.experimental.pallas import tpu as pltpu
from jax.sharding import PartitionSpec as P

NC = 16
UNROLL = 16
VMEM = pl.BlockSpec(memory_space=pltpu.VMEM)
SMEM = pl.BlockSpec(memory_space=pltpu.SMEM)
ANY = pl.BlockSpec(memory_space=pl.ANY)


def split(value):
    high = value.astype(jnp.bfloat16)
    low = (value - high.astype(jnp.float32)).astype(jnp.bfloat16)
    return high, low


def pack(words, keep, kind=0):
    words, keep = words.reshape(-1), keep.reshape(-1)
    slots = words.shape[0]
    spare = NC << 16
    number = jnp.arange(slots + UNROLL)
    rank = jnp.sum(keep[None, :] & (number[:slots, None] > number[None, :slots]), axis=1)
    count = jnp.sum(keep.astype(jnp.int32), keepdims=True)
    chosen = keep[None, :] & (rank[None, :] == number[:, None])
    packed = jnp.sum(jnp.where(chosen, words[None, :] - spare, 0), axis=1) + spare
    return jnp.concatenate([packed, count, jnp.full((1,), kind, jnp.int32)])


def contract_kernel(placed, n_left, n_right, words_ref, after_ref, *refs):
    left_refs, right_refs = refs[:n_left], refs[n_left : n_left + n_right]
    *before_ref, out_ref, left_raw, right_raw, total, sems = refs[n_left + n_right :]
    block, tile = right_refs[0].shape[0], right_refs[0].shape[-1]
    count, kind = (words_ref[words_ref.shape[0] - i] for i in (2, 1))
    del after_ref

    @pl.when(count > 0)
    def _():
        blocks = left_raw.shape[0] // block

        def lefts(act):
            for b, places in enumerate(placed):
                for at in sorted(set(places) - {None}):
                    here = functools.reduce(
                        jnp.logical_or, [kind == c for c, place in enumerate(places) if place == at]
                    )
                    copy = pltpu.make_async_copy(
                        left_refs[b], left_raw.at[pl.ds(at * block, block)], sems.at[at]
                    )
                    pl.when(here)(functools.partial(act, copy))

        rights = [
            pltpu.make_async_copy(ref, right_raw.at[pl.ds(k * block, block)], sems.at[blocks + k])
            for k, ref in enumerate(right_refs)
        ]
        lefts(lambda copy: copy.start())
        for copy in rights:
            copy.start()
        total[:NC] = before_ref[0][...] if before_ref else jnp.zeros_like(total[:NC])
        lefts(lambda copy: copy.wait())


        def some(i, ready):
            numbers = [words_ref[i * UNROLL + u] for u in range(UNROLL)]
            most = functools.reduce(jnp.maximum, [(word >> 8) & 255 for word in numbers])
            for k, copy in enumerate(rights):
                pl.when((ready <= k) & (most >= k * block))(copy.wait)
            products, targets = [], []
            for word in numbers:
                high, low = split(right_raw[(word >> 8) & 255])
                both = jnp.concatenate(
                    [
                        jnp.concatenate([high, low], axis=1),
                        jnp.concatenate([high, jnp.zeros_like(low)], axis=1),
                    ],
                    axis=0,
                )
                pair = jnp.concatenate(split(left_raw[word & 255]), axis=1)
                wide = jnp.dot(pair, both, preferred_element_type=jnp.float32)
                products.append(wide[:, :tile] + wide[:, tile:])
                targets.append(word >> 16)
            for product, target in zip(products, targets):
                total[target] += product
            return jnp.maximum(ready, sum(jnp.where(most >= k * block, 1, 0) for k in range(n_right)))

        ready = lax.fori_loop(0, (count + UNROLL - 1) // UNROLL, some, 0)
        for k, copy in enumerate(rights):
            pl.when(ready <= k)(copy.wait)
        out_ref[...] = total[:NC]

    @pl.when(count == 0)
    def _():
        out_ref[...] = before_ref[0][...] if before_ref else jnp.zeros_like(out_ref)


def contract(planned, lefts, rights, before=None, placed=None, after=None):
    block, tile = rights[0].shape[0], rights[0].shape[-1]
    placed = placed or [(b,) for b in range(len(lefts))]
    blocks = 1 + max(place for places in placed for place in places if place is not None)
    after = jnp.zeros((1,), jnp.int32) if after is None else after
    operands = [planned, after, *lefts, *rights] + ([] if before is None else [before])
    size = (blocks * block + len(rights) * block + 3 * NC + 1) * tile * tile
    return pl.pallas_call(
        functools.partial(contract_kernel, placed, len(lefts), len(rights)),
        out_shape=pltpu.VMEM((NC, tile, tile), jnp.float32),
        in_specs=[SMEM] * 2 + [ANY] * (len(lefts) + len(rights)) + [VMEM] * (before is not None),
        out_specs=VMEM,
        scratch_shapes=[
            pltpu.VMEM((blocks * block, tile, tile), jnp.float32),
            pltpu.VMEM((len(rights) * block, tile, tile), jnp.float32),
            pltpu.VMEM((NC + 1, tile, tile), jnp.float32),
            pltpu.SemaphoreType.DMA((blocks + len(rights),)),
        ],
        compiler_params=pltpu.CompilerParams(vmem_limit_bytes=4 * size + 4 * 2**20),
        cost_estimate=pl.CostEstimate(flops=1000, bytes_accessed=1000, transcendentals=0),
    )(*operands)


def probe(value):
    corner = value[(0,) * (value.ndim - 2) + (slice(0, 1), slice(0, 1))].reshape(1)
    return jnp.minimum(jnp.abs(corner), 0).astype(jnp.int32)


def ring(count, by):
    return [(i, (i + by) % count) for i in range(count)]


def general(own, lists):
    steps, tile = own.shape[0], own.shape[-1]
    panels = lax.axis_size("blk")
    whole = lax.all_gather(own, "rep", axis=0)
    total = None
    for step in range(steps):
        right = lax.ppermute(own, "blk", ring(panels, step)) if step else own
        word = lists[step, 0] | (lists[step, 1] << 8) | (lists[step, 2] << 16)
        total = contract(
            pack(word, lists[step, 2] < NC),
            [whole[:, step].reshape(-1, tile, tile)],
            [right.reshape(-1, tile, tile)],
            total,
        )
    return total


def on_a_line(own, lists):
    steps, per, tile = own.shape[0], own.shape[1], own.shape[-1]
    panels, slivers = lax.axis_size("blk"), lax.axis_size("rep")
    blk, rep = lax.axis_index("blk"), lax.axis_index("rep")
    even, odd, every = range(0, panels, 2), range(1, panels, 2), range(panels)
    inward, outward, across, beyond = [(0, 1), (3, 2)], [(1, 0), (2, 3)], [(1, 2), (2, 1)], [(0, 2), (3, 1)]
    here = [(i, i) for i in range(slivers)]
    middle = [(1, 1), (2, 2)]
    block = steps * per

    def send(value, *routes):
        pairs = [
            (b * slivers + source, (b + on) % panels * slivers + target)
            for these, ways, on in routes
            for b in these
            for source, target in ways
        ]
        return lax.ppermute(value, ("blk", "rep"), pairs)

    is_odd, is_middle = blk % 2 == 1, (rep == 1) | (rep == 2)
    full = is_middle | ~is_odd
    kind = 2 * is_odd.astype(jnp.int32) + 1 - is_middle.astype(jnp.int32)

    sliver = lists[:, 0] // per
    steps_of = jnp.arange(steps)[:, None]
    place = lists[:, 0] % per + per * steps_of + (lists[:, 1] << 8) + (lists[:, 2] << 16)
    live = lists[:, 2] < NC
    mine, beside, inner, outer = [
        sliver == i for i in (rep, rep ^ 1, jnp.where(rep < 2, 2, 1), jnp.where(rep < 2, 3, 0))
    ]

    def words(panel, *firsts):
        word = place + ((panel * block) << 8)
        for is_it, first in zip((mine, beside, inner, outer), firsts):
            word = word + jnp.where(is_it, first, 0)
        return word

    panel = jnp.where(is_odd, steps_of, jnp.array([0, 3, 2, 1])[:, None])
    own_words = pack(words(panel, 0, block, 2 * block, 3 * block), live & (mine | full), kind)
    their_words = pack(words(steps_of, 0, 0, block, 2 * block), live & is_odd & ~is_middle & ~mine)

    p1 = send(own, (even, beyond + outward, 0))
    p2 = send(own, (even, across, 0), (odd, inward, 0))
    p3 = send(own, (even, inward, 0), (odd, across, 0))
    two = send(own, (every, here, 2))
    their_words = send(their_words, (odd, inward, 0))
    alternate = send(own, (even, here, 1), (odd, here, 3))
    q1 = send(p2, (even, outward, 0), (odd, across, 0))
    q2 = send(jnp.where(is_middle, p1, two), (even, outward, 0), (even, inward, 1))
    h2 = send(p2, (odd, middle, 2))
    h1 = send(p3, (even, middle, 1))
    swapped = send(two, (even, here, 1), (odd, here, -1))

    own, p1, p2, p3, q1, q2, h1, h2, two, alternate, swapped = [
        x.reshape(-1, tile, tile) for x in (own, p1, p2, p3, q1, q2, h1, h2, two, alternate, swapped)
    ]
    late = probe(alternate)
    own, p1, p2, p3, two, q2, swapped, alternate = [
        pltpu.with_memory_space_constraint(x, pltpu.HBM)
        for x in (own, p1, p2, p3, two, q2, swapped, alternate)
    ]
    part = contract(their_words, [own, p3, q1], [p2, h1, h2, q2], after=late)
    part = send(part, (odd, outward, 0))

    lefts = [own, p1, p2, p3, q1, q2]
    placed = [
        (0, 0, 0, 0),
        (3, 1, None, None),
        (2, None, 1, None),
        (1, None, 2, None),
        (None, 2, 3, None),
        (None, 3, None, None),
    ]
    total = contract(own_words, lefts, [own, alternate, two, swapped], None, placed)
    return total + part


def per_device(p_tiles, tasks):
    own, lists = p_tiles[0, 0], tasks[0, 0]
    small = lax.axis_size("rep") == 4 and own.shape[0] == 4 and lax.axis_size("blk") % 2 == 0
    return (on_a_line if small else general)(own, lists)[None, None]


def solution(mesh):
    return jax.shard_map(
        per_device,
        mesh=mesh,
        in_specs=(P("blk", "rep", None, None, None, None), P("blk", "rep", None, None, None)),
        out_specs=P("blk", "rep", None, None, None),
        check_vma=False,
    )
```
